32 devices in a mesh: ctx: 8 (over z, y), tp: 4 (over x, core).
Axes of the slice: x: 2, y: 2, z: 4, core: 2. Of those that a mesh axis runs over, the one named last changes fastest.
Arguments:
- queries: bfloat16 [4096, 2048], P('ctx', 'tp'), may hold values from -7 to 7
- keys: bfloat16 [4096, 2048], P('ctx', 'tp'), may hold values from -6 to 6
- values: bfloat16 [4096, 2048], P('ctx', 'tp'), may hold values from -6 to 6
- doc_ids: int32 [32], replicated, may hold values from 0 to 3, never falling along the last dimension, each value on 1 to 20 neighbouring positions
- span_start: int32 [4], replicated, may hold values from 0 to 31, as said below
- span_end: int32 [4], replicated, may hold values from 1 to 32, as said below
- out_weight: bfloat16 [2048, 4096], P('tp'), may hold values from -0.125 to 0.125
Outputs:
- mixed: bfloat16 [4096, 4096], P(('ctx', 'tp'))
The draws below stay inside these ranges and needn't reach their ends.
Inputs may be any that keep to these rules, and one draw needn't show every extreme that they name: `doc_ids`: each document occupies consecutive blocks. Spans are disjoint and in increasing order; span s covers blocks span_start[s] to span_end[s] - 1. span_end[s] - span_start[s] is 1 to 4.
All inputs are finite; a program needn't handle non-finite values.
Results may differ from the reference program's by a relative error of at most 0.012.
Values may be sent and summed in bfloat16 or wider, within the bound.
A program may use at most 128 MiB of HBM per device.

```python
import math
import jax
import jax.numpy as jnp
import numpy as np
from jax import lax

D = 4096
HEADS = 16
HEAD_DIM = 128
BLOCK = 128
SEQ = 4096
NB = 32
NDOC = 4
DOC_MOST = 20


def attention_pair(key):
    base = jax.random.fold_in(key, 5)
    key_one, key_two = jax.random.split(base, 2)
    shape = (SEQ, HEADS * HEAD_DIM)
    query_draw = jnp.clip(jax.random.normal(key_one, shape, jnp.float32), -6.0, 6.0)
    key_draw = jnp.clip(jax.random.normal(key_two, shape, jnp.float32), -6.0, 6.0)
    return (query_draw, key_draw)


def draw_queries(key, part):
    return attention_pair(key)[0].astype(jnp.bfloat16)


def draw_keys(key, part):
    return attention_pair(key)[1].astype(jnp.bfloat16)


def span_pair(key):
    base = jax.random.fold_in(key, 11)
    key_offset, key_length = jax.random.split(base)
    groups = NB // 8
    offset = jax.random.randint(key_offset, (groups,), 0, 4)
    length = jax.random.randint(key_length, (groups,), 1, 5)
    group = jnp.arange(groups, dtype=jnp.int32)
    offset = jnp.where(group == 0, 0, offset)
    length = jnp.where(group == 0, 4, length)
    start = 8 * group + offset
    start = jnp.where(group == groups - 1, 8 * group + 8 - length, start)
    return (start.astype(jnp.int32), (start + length).astype(jnp.int32))


def draw_span_start(key, part):
    return span_pair(key)[0]


def draw_span_end(key, part):
    return span_pair(key)[1]


def level_of(stream_key, shape, shards, least, high):
    def one(position, parts):
        heights = jax.random.uniform(jax.random.fold_in(jax.random.fold_in(stream_key, 6), position), (parts,), jnp.float32, least / len(shards), high / len(shards))
        return jnp.repeat(jnp.exp(heights), shape[position] // parts).reshape((-1,) + (1,) * (len(shape) - position - 1))

    level = one(*shards[0])
    for cut in shards[1:]:
        level = level * one(*cut)
    return level


def split_up(count, total, bound, slope):
    loads = [(1 << 20) // math.isqrt(grade ** slope) + 1 for grade in range(2, count + 1)]
    rest, counts = total - bound - (count - 1), [1] * (count - 1)
    while rest > 0:
        candidates = [i for i in range(count - 1) if counts[i] < bound]
        mass, remaining = sum([loads[i] for i in candidates]), rest
        for i in candidates:
            addition = min(bound - counts[i], max(1, remaining * loads[i] // mass), rest)
            counts[i] = counts[i] + addition
            rest = rest - addition
    return np.array([bound] + counts)


def ragged_sizes(stream_key, amount, total, most, slope):
    if amount == 2:
        one = jax.random.randint(stream_key, (), max(1, total - most), min(most, total - 1) + 1)
        return jnp.stack([one, total - one])
    lengths = jnp.asarray(split_up(amount, total, most, slope), jnp.int32)
    twos = (amount - 1) // 2
    donor, receiver = lengths[1:1 + 2 * twos:2], lengths[2:2 + 2 * twos:2]
    room = jnp.minimum(donor - 1, most - receiver)
    moved = jax.random.randint(jax.random.fold_in(stream_key, 1), (twos,), 0, 1 << 20) % (room + 1)
    lengths = lengths.at[1:1 + 2 * twos:2].set(donor - moved).at[2:2 + 2 * twos:2].set(receiver + moved)
    return lengths[jax.random.permutation(jax.random.fold_in(stream_key, 2), amount)]


def scatter_about(stream_key, shape, scale, bound, cuts=(), held_as=jnp.bfloat16):
    entries = jax.random.normal(stream_key, shape, jnp.float32) * scale
    if len(cuts) > 0:
        entries = level_of(stream_key, shape, cuts, -0.22, 0.18) * entries
    return jnp.clip(entries, min=-bound, max=bound).astype(held_as)


def setup_inputs(seed: int = 0) -> dict:
    key_list = jax.random.split(jax.random.key(seed), 8)
    return {
        "queries": draw_queries(jax.random.fold_in(key_list[7], 71), 0),
        "keys": draw_keys(jax.random.fold_in(key_list[7], 71), 0),
        "values": scatter_about(key_list[2], (SEQ, HEADS * HEAD_DIM), 1.0, 6.0, ((0, 8), (1, 4))),
        "doc_ids": jnp.searchsorted(jnp.cumsum(ragged_sizes(key_list[3], NDOC, NB, DOC_MOST, 2)), jnp.arange(NB), side="right").astype(jnp.int32),
        "span_start": draw_span_start(jax.random.fold_in(key_list[7], 71), 0),
        "span_end": draw_span_end(jax.random.fold_in(key_list[7], 71), 0),
        "out_weight": scatter_about(key_list[6], (HEADS * HEAD_DIM, D), (HEADS * HEAD_DIM) ** -0.5, 0.125, ((0, 4),)),
    }


NEG = -1e+30

def block_spans(span_start, span_end, count):
    blocks = jnp.arange(count, dtype=jnp.int32)
    inside = (blocks[:, None] >= span_start[None, :]) & (blocks[:, None] < span_end[None, :])
    labels = jnp.arange(1, span_start.shape[0] + 1, dtype=jnp.int32)
    return lax.optimization_barrier(jnp.sum(jnp.where(inside, labels[None, :], 0), axis=1)).astype(jnp.int32) - 1

def reference(queries, keys, values, doc_ids, span_start, span_end, out_weight):
    seq_len = queries.shape[0]
    block_count = seq_len // BLOCK
    span_blocks = block_spans(span_start, span_end, block_count)
    positions = jnp.arange(seq_len, dtype=jnp.int32)
    doc_tok = doc_ids[positions // BLOCK]
    span_tok = span_blocks[positions // BLOCK]
    key_heads = keys.astype(jnp.float32).reshape(seq_len, HEADS, HEAD_DIM)
    value_heads = values.astype(jnp.float32).reshape(seq_len, HEADS, HEAD_DIM)
    scale = 1.0 / math.sqrt(HEAD_DIM)

    def one_block(index):
        first = (index * BLOCK).astype(jnp.int32)
        query_heads = lax.dynamic_slice_in_dim(queries, first, BLOCK, 0).astype(jnp.float32).reshape(BLOCK, HEADS, HEAD_DIM)
        query_pos = first + jnp.arange(BLOCK, dtype=jnp.int32)
        query_doc = lax.dynamic_slice_in_dim(doc_tok, first, BLOCK, 0)
        query_span = lax.dynamic_slice_in_dim(span_tok, first, BLOCK, 0)
        allowed = (query_doc[:, None] == doc_tok[None, :]) & ((positions[None, :] <= query_pos[:, None]) | (query_span[:, None] == span_tok[None, :]) & (query_span[:, None] >= 0))
        scores = jnp.einsum('qhd,khd->hqk', query_heads, key_heads) * scale
        scores = jnp.where(allowed[None], scores, NEG)
        row_max = lax.optimization_barrier(jnp.max(scores, axis=2, keepdims=True))
        weights = jnp.where(allowed[None], jnp.exp(scores - row_max), 0.0)
        totals = lax.optimization_barrier(jnp.sum(weights, axis=2))
        rounded = lax.optimization_barrier(weights.astype(jnp.bfloat16)).astype(jnp.float32)
        attended = jnp.einsum('hqk,khd->qhd', rounded, value_heads) / totals.T[:, :, None]
        return attended.reshape(BLOCK, HEADS * HEAD_DIM).astype(jnp.bfloat16)
    attended = lax.map(one_block, jnp.arange(block_count, dtype=jnp.int32)).reshape(seq_len, HEADS * HEAD_DIM)
    return jnp.dot(attended, out_weight, preferred_element_type=jnp.float32).astype(jnp.bfloat16)
```

```python
import functools
import math

import jax
import jax.numpy as jnp
from jax import lax
from jax.experimental import pallas as pl
from jax.experimental.pallas import tpu as pltpu
from jax.sharding import PartitionSpec as P

HEAD_DIM = 128
BLOCK = 128
NEG = -1e30
FLOOR = -1e29
MESH = pl.DeviceIdType.MESH
TAIL = 8


def kernel(
    levels, reach, doc_ref, start_ref, end_ref, q_ref, k_ref, v_ref, w_ref, out_ref,
    qbuf, kbuf, vbuf, kla, vla, lim, limla, part, stat, acc_s, acc_r, st_s, st_r, att, attq,
    wbuf, pbuf, keep, send1, recv1, send2, recv2,
    bar_q_s, q_r, kv_s, kv_r, la_s, la_r, o_s, o_r, s_s, s_r, loc, wsem, e1s, e1r, e2s, e2r,
):
    heads = qbuf.shape[1]
    rows = qbuf.shape[2]
    nb = rows // BLOCK
    depth = qbuf.shape[0]
    nspan = start_ref.shape[0]
    me = lax.axis_index("ctx")
    tp = lax.axis_index("tp")
    r, c = me // 2, me % 2
    a, core = tp // 2, tp % 2
    most = (reach + 1 - c) // 2
    const = math.log2(math.e) / math.sqrt(HEAD_DIM)

    up, down, side = (me + 2, tp), (me - 2, tp), (me + 1 - 2 * c, tp)
    mate, across = (me, tp + 1 - 2 * core), (me, tp + 2 - 4 * a)
    has_up, has_down = r < levels - 1, r > 0
    gives = (c == 0) & (r > 0)
    takes = (c == 1) & (r < levels - 1)

    barrier = pltpu.get_barrier_semaphore()
    for other in (side, mate, across):
        pl.semaphore_signal(barrier, inc=1, device_id=other, device_id_type=MESH)
    for cond, other in ((has_up, up), (has_down, down), (gives, (me - 1, tp)), (takes, (me + 1, tp))):
        @pl.when(cond)
        def _(other=other):
            pl.semaphore_signal(barrier, inc=1, device_id=other, device_id_type=MESH)

    w_copy = pltpu.make_async_copy(w_ref, wbuf, wsem)

    def cols(h):
        return pl.ds(pl.multiple_of(h * HEAD_DIM, HEAD_DIM), HEAD_DIM)

    mine = pl.ds(pl.multiple_of(c * rows, rows), rows)
    look = kla.shape[1]

    def local(j, h):
        src = (q_ref.at[:, cols(h)], k_ref.at[:, cols(h)], v_ref.at[:, cols(h)])[j]
        dst = (qbuf.at[0, h], kbuf.at[h, mine], vbuf.at[h, mine])[j]
        return pltpu.make_async_copy(src, dst, loc.at[j, h])

    def remote(src, dst, ss, rs, dev):
        return pltpu.make_async_remote_copy(
            src_ref=src, dst_ref=dst, send_sem=ss, recv_sem=rs, device_id=dev, device_id_type=MESH
        )

    def k_side(h):
        return remote(k_ref.at[:, cols(h)], kbuf.at[h, mine], kv_s.at[0, h], kv_r.at[0, h], side)

    def v_side(h):
        return remote(v_ref.at[:, cols(h)], vbuf.at[h, mine], kv_s.at[1, h], kv_r.at[1, h], side)

    def k_look(h):
        return remote(
            k_ref.at[pl.ds(0, look), cols(h)], kla.at[h], la_s.at[0, h], la_r.at[0, h], (me - 1, tp)
        )

    def v_look(h):
        return remote(
            v_ref.at[pl.ds(0, look), cols(h)], vla.at[h], la_s.at[1, h], la_r.at[1, h], (me - 1, tp)
        )

    def q_own(h):
        return remote(q_ref.at[:, cols(h)], qbuf.at[1, h], bar_q_s.at[0, h], q_r.at[1, h], down)

    def q_pass(j, h):
        return remote(qbuf.at[j, h], qbuf.at[j + 1, h], bar_q_s.at[j, h], q_r.at[j + 1, h], down)

    def o_up(j, h):
        return remote(acc_s.at[j, h], acc_r.at[j - 1, h], o_s.at[j, h], o_r.at[j - 1, h], up)

    def s_up(j, h):
        return remote(st_s.at[j, h], st_r.at[j - 1, h], s_s.at[j, h], s_r.at[j - 1, h], up)

    def valid(j):
        return (r + j < levels) & (j <= most)

    def below(j):
        return has_down & (j + 1 <= most)

    @pl.loop(0, heads)
    def _(h):
        for j in range(3):
            local(j, h).start()

    w_copy.start()
    total = 3 + sum(x.astype(jnp.int32) for x in (has_up, has_down, gives, takes))
    pl.semaphore_wait(barrier, total)

    @pl.loop(0, heads)
    def _(h):
        k_side(h).start()

        @pl.when(below(0))
        def _():
            q_own(h).start()

        v_side(h).start()

        @pl.when(gives)
        def _():
            k_look(h).start()
            v_look(h).start()

    def span_of(b):
        total = jnp.int32(-1)
        for s in range(nspan):
            total = jnp.where((b >= start_ref[s]) & (b < end_ref[s]), jnp.int32(s), total)
        return total

    lane = lax.broadcasted_iota(jnp.int32, (1, rows), 1)

    def row_of(values):
        row = jnp.full((1, rows), values[0], jnp.int32)
        for n in range(1, nb):
            row = jnp.where(lane >= n * BLOCK, values[n], row)
        return row

    def limit(qdoc, qspan, qpos, kb):
        kd, ks = doc_ref[kb], span_of(kb)
        reachable = jnp.where((qspan == ks) & (qspan >= 0), BLOCK, qpos - kb * BLOCK)
        return jnp.where(qdoc == kd, reachable, -1)

    @pl.loop(0, depth)
    def _(j):
        @pl.when(valid(j))
        def _():
            qi = me + 2 * j
            qdoc = row_of([doc_ref[qi * nb + n] for n in range(nb)])
            qspan = row_of([span_of(qi * nb + n) for n in range(nb)])
            qpos = lane + qi * rows
            for n in range(2 * nb):
                lim[j, n] = limit(qdoc, qspan, qpos, 2 * r * nb + n)

            @pl.when((j == 0) & takes)
            def _():
                for n in range(look // BLOCK):
                    limla[n] = limit(qdoc, qspan, qpos, (me + 1) * nb + n)

    def piece(q, kmat, vmat, limits):
        s = lax.dot_general(kmat, q, (((1,), (1,)), ((), ())), preferred_element_type=jnp.float32)
        n = s.shape[0] // BLOCK
        s = s.reshape(n, BLOCK, rows)
        place = lax.broadcasted_iota(jnp.int32, (n, BLOCK, rows), 1)
        s = jnp.where(place <= limits, s, NEG)
        m = jnp.maximum(jnp.max(jnp.max(s, axis=0), axis=0, keepdims=True), FLOOR)
        p = jnp.exp2((s - m[None]) * const)
        l = jnp.sum(jnp.sum(p, axis=0), axis=0, keepdims=True)
        p = p.astype(jnp.bfloat16).reshape(n * BLOCK, rows)
        o = lax.dot_general(vmat, p, (((0,), (0,)), ((), ())), preferred_element_type=jnp.float32)
        return o, m, l

    def merge(j, h, o, m, l, scale_o):
        om, ol = stat[j, h, 0:1], stat[j, h, 1:2]
        top = jnp.maximum(m, om)
        f_new = jnp.exp2((m - top) * const)
        f_old = jnp.exp2((om - top) * const)
        part[j, h] = part[j, h] * f_old + o * (f_new * scale_o)
        stat[j, h, 0:1] = top
        stat[j, h, 1:2] = ol * f_old + l * f_new

    @pl.loop(0, heads + 1)
    def _(step):
        @pl.when(step < heads)
        def _():
            h = step

            @pl.loop(1, depth)
            def _(j):
                @pl.when(valid(j))
                def _():
                    remote(qbuf.at[j, h], qbuf.at[j, h], bar_q_s.at[j, h], q_r.at[j, h], up).wait_recv()

                    @pl.when(below(j))
                    def _():
                        q_pass(j, h).start()

            for j in range(3):
                local(j, h).wait()
            k_side(h).wait_recv()
            v_side(h).wait_recv()

            @pl.loop(0, depth)
            def _(j):
                @pl.when(valid(j))
                def _():
                    o, m, l = piece(qbuf[j, h], kbuf[h], vbuf[h], lim[j])
                    part[j, h] = o
                    stat[j, h, 0:1] = m
                    stat[j, h, 1:2] = l

            @pl.when(takes)
            def _():
                k_look(h).wait_recv()
                v_look(h).wait_recv()
                o, m, l = piece(qbuf[0, h], kla[h], vla[h], limla[...])
                merge(0, h, o, m, l, 1.0)

        hf = jnp.where(has_down, step - 1, step)

        @pl.when((hf >= 0) & (hf < heads))
        def _():
            @pl.loop(0, depth)
            def _(j):
                @pl.when(valid(j))
                def _():
                    @pl.when(below(j))
                    def _():
                        remote(acc_s.at[j, hf], acc_r.at[j, hf], o_s.at[j, hf], o_r.at[j, hf], down).wait_recv()
                        remote(st_s.at[j, hf], st_r.at[j, hf], s_s.at[j, hf], s_r.at[j, hf], down).wait_recv()
                        m, l = st_r[j, hf, 0:1], st_r[j, hf, 1:2]
                        merge(j, hf, acc_r[j, hf].astype(jnp.float32), m, l, l)

                    l = stat[j, hf, 1:2]
                    o = (part[j, hf] * (1.0 / jnp.where(l > 0.0, l, 1.0))).astype(jnp.bfloat16)

                    @pl.when(j == 0)
                    def _():
                        att[hf] = o

                    @pl.when(j > 0)
                    def _():
                        acc_s[j, hf] = o
                        st_s[j, hf] = stat[j, hf]
                        o_up(j, hf).start()
                        s_up(j, hf).start()

    w_copy.wait()
    attq[...] = att[...].reshape(heads * HEAD_DIM, rows).T
    wide = pbuf.shape[2]
    piece_rows = pbuf.shape[1]
    chunks = keep.shape[0]

    def to_mate(n):
        return remote(send1.at[n], recv1.at[n], e1s.at[n], e1r.at[n], mate)

    def to_across(n):
        return remote(send2.at[n], recv2.at[n], e2s.at[n], e2r.at[n], across)

    def span(n):
        return pl.ds(pl.multiple_of(n * wide, wide), wide)

    @pl.loop(0, chunks + 1)
    def _(step):
        @pl.when(step < chunks)
        def _():
            n = step
            full = jnp.dot(attq[...], wbuf[:, span(n)], preferred_element_type=jnp.float32)
            pbuf[...] = full.reshape(4, piece_rows, wide)
            for t in range(2):
                send1[n, t] = pbuf[2 * t + 1 - core].astype(jnp.bfloat16)
                keep[n, t] = pbuf[2 * t + core]
            to_mate(n).start()

        @pl.when(step > 0)
        def _():
            n = step - 1
            to_mate(n).wait_recv()
            far = keep[n, 1 - a] + recv1[n, 1 - a].astype(jnp.float32)
            send2[n] = far.astype(jnp.bfloat16)
            to_across(n).start()

    @pl.loop(0, chunks)
    def _(n):
        to_across(n).wait_recv()
        near = keep[n, a] + recv1[n, a].astype(jnp.float32) + recv2[n].astype(jnp.float32)
        out_ref[:, span(n)] = near.astype(out_ref.dtype)

    @pl.loop(0, chunks)
    def _(n):
        to_mate(n).wait_send()
        to_across(n).wait_send()

    @pl.loop(0, heads)
    def _(h):
        k_side(h).wait_send()
        v_side(h).wait_send()

        @pl.when(below(0))
        def _():
            q_own(h).wait_send()

        @pl.when(gives)
        def _():
            k_look(h).wait_send()
            v_look(h).wait_send()

        @pl.loop(1, depth)
        def _(j):
            @pl.when(valid(j))
            def _():
                o_up(j, h).wait_send()
                s_up(j, h).wait_send()

                @pl.when(below(j))
                def _():
                    q_pass(j, h).wait_send()


def solution(mesh):
    n_ctx, n_tp = mesh.shape["ctx"], mesh.shape["tp"]

    def per_device(queries, keys, values, doc_ids, span_start, span_end, out_weight):
        rows, width = queries.shape
        heads = width // HEAD_DIM
        blocks = doc_ids.shape[0]
        nb = rows // BLOCK
        longest = blocks * 5 // 8
        reach = min(-(-(longest - 1) // nb), n_ctx - 1)
        levels = n_ctx // 2
        depth = min((reach + 1) // 2, levels - 1) + 1
        model = out_weight.shape[1]
        chunks = TAIL
        wide = model // chunks
        piece = rows // n_tp
        bf, f32, i32 = jnp.bfloat16, jnp.float32, jnp.int32
        dma = pltpu.SemaphoreType.DMA
        look = 3 * BLOCK
        smem = pl.BlockSpec(memory_space=pltpu.SMEM)
        anym = pl.BlockSpec(memory_space=pl.ANY)
        flops = 4 * rows * rows * 2 * width * depth + 2 * rows * width * model
        return pl.pallas_call(
            functools.partial(kernel, levels, reach),
            out_shape=jax.ShapeDtypeStruct((piece, model), bf),
            in_specs=[smem, smem, smem, anym, anym, anym, anym],
            out_specs=pl.BlockSpec(memory_space=pltpu.VMEM),
            scratch_shapes=[
                pltpu.VMEM((depth, heads, rows, HEAD_DIM), bf),
                pltpu.VMEM((heads, 2 * rows, HEAD_DIM), bf),
                pltpu.VMEM((heads, 2 * rows, HEAD_DIM), bf),
                pltpu.VMEM((heads, look, HEAD_DIM), bf),
                pltpu.VMEM((heads, look, HEAD_DIM), bf),
                pltpu.VMEM((depth, 2 * nb, 1, rows), i32),
                pltpu.VMEM((3, 1, rows), i32),
                pltpu.VMEM((depth, heads, HEAD_DIM, rows), f32),
                pltpu.VMEM((depth, heads, 8, rows), f32),
                pltpu.VMEM((depth, heads, HEAD_DIM, rows), bf),
                pltpu.VMEM((depth, heads, HEAD_DIM, rows), bf),
                pltpu.VMEM((depth, heads, 8, rows), f32),
                pltpu.VMEM((depth, heads, 8, rows), f32),
                pltpu.VMEM((heads, HEAD_DIM, rows), bf),
                pltpu.VMEM((rows, width), bf),
                pltpu.VMEM(out_weight.shape, bf),
                pltpu.VMEM((4, piece, wide), f32),
                pltpu.VMEM((chunks, 2, piece, wide), f32),
                pltpu.VMEM((chunks, 2, piece, wide), bf),
                pltpu.VMEM((chunks, 2, piece, wide), bf),
                pltpu.VMEM((chunks, piece, wide), bf),
                pltpu.VMEM((chunks, piece, wide), bf),
                dma((depth, heads)), dma((depth, heads)),
                dma((2, heads)), dma((2, heads)),
                dma((2, heads)), dma((2, heads)),
                dma((depth, heads)), dma((depth, heads)),
                dma((depth, heads)), dma((depth, heads)),
                dma((3, heads)), dma,
                dma((chunks,)), dma((chunks,)),
                dma((chunks,)), dma((chunks,)),
            ],
            compiler_params=pltpu.CompilerParams(
                collective_id=0, has_side_effects=True, vmem_limit_bytes=60 * 1024 * 1024
            ),
            cost_estimate=pl.CostEstimate(
                flops=flops, bytes_accessed=8 * 1024 * 1024, transcendentals=0
            ),
        )(doc_ids, span_start, span_end, queries, keys, values, out_weight)

    return jax.shard_map(
        per_device,
        mesh=mesh,
        in_specs=(P("ctx", "tp"), P("ctx", "tp"), P("ctx", "tp"), P(), P(), P(), P("tp", None)),
        out_specs=P(("ctx", "tp"), None),
        check_vma=False,
    )
```

```python
import functools
import math

import jax
import jax.numpy as jnp
from jax import lax
from jax.experimental import pallas as pl
from jax.experimental.pallas import tpu as pltpu
from jax.sharding import PartitionSpec as P

HEAD_DIM = 128
BLOCK = 128
NEG = -1e30
FLOOR = -1e29
MESH = pl.DeviceIdType.MESH
TAIL = 8


def kernel(
    levels, reach, doc_ref, start_ref, end_ref, q_ref, k_ref, v_ref, w_ref, out_ref,
    qbuf, kbuf, vbuf, kla, vla, lim, limla, part, stat, acc_s, acc_r, st_s, st_r, att, attq,
    wbuf, pbuf, keep, send1, recv1, send2, recv2, sbuf, wts, vt,
    bar_q_s, q_r, kv_s, kv_r, la_s, la_r, o_s, o_r, s_s, s_r, loc, wsem, e1s, e1r, e2s, e2r,
):
    heads = qbuf.shape[1]
    rows = qbuf.shape[2]
    nb = rows // BLOCK
    depth = qbuf.shape[0]
    nspan = start_ref.shape[0]
    me = lax.axis_index("ctx")
    tp = lax.axis_index("tp")
    r, c = me // 2, me % 2
    a, core = tp // 2, tp % 2
    most = (reach + 1 - c) // 2
    const = math.log2(math.e) / math.sqrt(HEAD_DIM)

    up, down, side = (me + 2, tp), (me - 2, tp), (me + 1 - 2 * c, tp)
    mate, across = (me, tp + 1 - 2 * core), (me, tp + 2 - 4 * a)
    has_up, has_down = r < levels - 1, r > 0
    gives = (c == 0) & (r > 0)
    takes = (c == 1) & (r < levels - 1)

    barrier = pltpu.get_barrier_semaphore()
    for other in (side, mate, across):
        pl.semaphore_signal(barrier, inc=1, device_id=other, device_id_type=MESH)
    for cond, other in ((has_up, up), (has_down, down), (gives, (me - 1, tp)), (takes, (me + 1, tp))):
        @pl.when(cond)
        def _(other=other):
            pl.semaphore_signal(barrier, inc=1, device_id=other, device_id_type=MESH)

    w_copy = pltpu.make_async_copy(w_ref, wbuf, wsem)

    def cols(h):
        return pl.ds(pl.multiple_of(h * HEAD_DIM, HEAD_DIM), HEAD_DIM)

    mine = pl.ds(pl.multiple_of(c * rows, rows), rows)
    look = kla.shape[1]

    def local(j, h):
        src = (q_ref.at[:, cols(h)], k_ref.at[:, cols(h)], v_ref.at[:, cols(h)])[j]
        dst = (qbuf.at[0, h], kbuf.at[h, mine], vbuf.at[h, mine])[j]
        return pltpu.make_async_copy(src, dst, loc.at[j, h])

    def remote(src, dst, ss, rs, dev):
        return pltpu.make_async_remote_copy(
            src_ref=src, dst_ref=dst, send_sem=ss, recv_sem=rs, device_id=dev, device_id_type=MESH
        )

    def k_side(h):
        return remote(k_ref.at[:, cols(h)], kbuf.at[h, mine], kv_s.at[0, h], kv_r.at[0, h], side)

    def v_side(h):
        return remote(v_ref.at[:, cols(h)], vbuf.at[h, mine], kv_s.at[1, h], kv_r.at[1, h], side)

    def k_look(h):
        return remote(
            k_ref.at[pl.ds(0, look), cols(h)], kla.at[h], la_s.at[0, h], la_r.at[0, h], (me - 1, tp)
        )

    def v_look(h):
        return remote(
            v_ref.at[pl.ds(0, look), cols(h)], vla.at[h], la_s.at[1, h], la_r.at[1, h], (me - 1, tp)
        )

    def q_own(h):
        return remote(q_ref.at[:, cols(h)], qbuf.at[1, h], bar_q_s.at[0, h], q_r.at[1, h], down)

    def q_pass(j, h):
        return remote(qbuf.at[j, h], qbuf.at[j + 1, h], bar_q_s.at[j, h], q_r.at[j + 1, h], down)

    def o_up(j, h):
        return remote(acc_s.at[j, h], acc_r.at[j - 1, h], o_s.at[j, h], o_r.at[j - 1, h], up)

    def s_up(j, h):
        return remote(st_s.at[j, h], st_r.at[j - 1, h], s_s.at[j, h], s_r.at[j - 1, h], up)

    def valid(j):
        return (r + j < levels) & (j <= most)

    def below(j):
        return has_down & (j + 1 <= most)

    @pl.loop(0, heads)
    def _(h):
        for j in range(3):
            local(j, h).start()

    w_copy.start()
    total = 3 + sum(x.astype(jnp.int32) for x in (has_up, has_down, gives, takes))
    pl.semaphore_wait(barrier, total)

    @pl.loop(0, heads)
    def _(h):
        k_side(h).start()

        @pl.when(below(0))
        def _():
            q_own(h).start()

        v_side(h).start()

        @pl.when(gives)
        def _():
            k_look(h).start()
            v_look(h).start()

    def span_of(b):
        total = jnp.int32(-1)
        for s in range(nspan):
            total = jnp.where((b >= start_ref[s]) & (b < end_ref[s]), jnp.int32(s), total)
        return total

    lane = lax.broadcasted_iota(jnp.int32, (1, rows), 1)

    def row_of(values):
        row = jnp.full((1, rows), values[0], jnp.int32)
        for n in range(1, nb):
            row = jnp.where(lane >= n * BLOCK, values[n], row)
        return row

    def limit(qdoc, qspan, qpos, kb):
        kd, ks = doc_ref[kb], span_of(kb)
        reachable = jnp.where((qspan == ks) & (qspan >= 0), BLOCK, qpos - kb * BLOCK)
        return jnp.where(qdoc == kd, reachable, -1)

    @pl.loop(0, depth)
    def _(j):
        @pl.when(valid(j))
        def _():
            qi = me + 2 * j
            qdoc = row_of([doc_ref[qi * nb + n] for n in range(nb)])
            qspan = row_of([span_of(qi * nb + n) for n in range(nb)])
            qpos = lane + qi * rows
            for n in range(2 * nb):
                lim[j, n] = limit(qdoc, qspan, qpos, 2 * r * nb + n)

            @pl.when((j == 0) & takes)
            def _():
                for n in range(look // BLOCK):
                    limla[n] = limit(qdoc, qspan, qpos, (me + 1) * nb + n)

    half = rows // 2

    def piece(j, h, k_at, vt_at, lim_at, count):
        for side_q in range(2):
            lanes = slice(side_q * half, (side_q + 1) * half)
            q = qbuf[j, h, lanes, :]
            top = None
            for n in range(count):
                s = lax.dot_general(
                    k_at(n), q, (((1,), (1,)), ((), ())), preferred_element_type=jnp.float32
                )
                place = lax.broadcasted_iota(jnp.int32, (BLOCK, half), 0)
                s = jnp.where(place <= lim_at(n, lanes), s, NEG)
                sbuf[n, :, lanes] = s
                most_here = jnp.max(s.reshape(BLOCK // 8, 8, half), axis=0)
                top = most_here if top is None else jnp.maximum(top, most_here)
            m = jnp.maximum(jnp.max(top, axis=0, keepdims=True), FLOOR)
            shift = m * const
            total = jnp.zeros((8, half), jnp.float32)
            for n in range(count):
                p = jnp.exp2(sbuf[n, :, lanes] * const - shift)
                total = total + jnp.sum(p.reshape(BLOCK // 8, 8, half), axis=0)
                wts[n * BLOCK : (n + 1) * BLOCK, lanes] = p.astype(jnp.bfloat16)
            l = jnp.sum(total, axis=0, keepdims=True)
            o = jnp.dot(vt_at(), wts[: count * BLOCK, lanes], preferred_element_type=jnp.float32)
            yield lanes, o, m, l

    def merge(j, h, lanes, o, m, l, scale_o):
        om, ol = stat[j, h, 0:1, lanes], stat[j, h, 1:2, lanes]
        top = jnp.maximum(m, om)
        f_new = jnp.exp2((m - top) * const)
        f_old = jnp.exp2((om - top) * const)
        part[j, h, :, lanes] = part[j, h, :, lanes] * f_old + o * (f_new * scale_o)
        stat[j, h, 0:1, lanes] = top
        stat[j, h, 1:2, lanes] = ol * f_old + l * f_new

    def put(j, h, results):
        for lanes, o, m, l in results:
            part[j, h, :, lanes] = o
            stat[j, h, 0:1, lanes] = m
            stat[j, h, 1:2, lanes] = l

    @pl.loop(0, heads + 1)
    def _(step):
        @pl.when(step < heads)
        def _():
            h = step

            @pl.loop(1, depth)
            def _(j):
                @pl.when(valid(j))
                def _():
                    remote(qbuf.at[j, h], qbuf.at[j, h], bar_q_s.at[j, h], q_r.at[j, h], up).wait_recv()

                    @pl.when(below(j))
                    def _():
                        q_pass(j, h).start()

            for j in range(3):
                local(j, h).wait()
            k_side(h).wait_recv()
            v_side(h).wait_recv()

            vt[...] = vbuf[h].T

            @pl.loop(0, depth)
            def _(j):
                far = 2 * j + c > reach

                def block(first):
                    return lambda n: kbuf[h, (first + n) * BLOCK : (first + n + 1) * BLOCK, :]

                @pl.when(valid(j) & jnp.logical_not(far))
                def _():
                    put(j, h, piece(
                        j, h, block(0), lambda: vt[...], lambda n, lanes: lim[j, n, :, lanes], 2 * nb
                    ))

                @pl.when(valid(j) & far)
                def _():
                    put(j, h, piece(
                        j, h, block(nb), lambda: vt[:, rows:],
                        lambda n, lanes: lim[j, nb + n, :, lanes], nb
                    ))

            @pl.when(takes)
            def _():
                k_look(h).wait_recv()
                v_look(h).wait_recv()
                vt[:, :look] = vla[h].T
                for lanes, o, m, l in piece(
                    0, h, lambda n: kla[h, n * BLOCK : (n + 1) * BLOCK, :], lambda: vt[:, :look],
                    lambda n, lanes: limla[n, :, lanes], look // BLOCK
                ):
                    merge(0, h, lanes, o, m, l, 1.0)

        hf = jnp.where(has_down, step - 1, step)

        @pl.when((hf >= 0) & (hf < heads))
        def _():
            @pl.loop(0, depth)
            def _(j):
                @pl.when(valid(j))
                def _():
                    @pl.when(below(j))
                    def _():
                        remote(acc_s.at[j, hf], acc_r.at[j, hf], o_s.at[j, hf], o_r.at[j, hf], down).wait_recv()
                        remote(st_s.at[j, hf], st_r.at[j, hf], s_s.at[j, hf], s_r.at[j, hf], down).wait_recv()
                        m, l = st_r[j, hf, 0:1], st_r[j, hf, 1:2]
                        merge(j, hf, slice(None), acc_r[j, hf].astype(jnp.float32), m, l, l)

                    l = stat[j, hf, 1:2]
                    o = (part[j, hf] * (1.0 / jnp.where(l > 0.0, l, 1.0))).astype(jnp.bfloat16)

                    @pl.when(j == 0)
                    def _():
                        att[hf] = o

                    @pl.when(j > 0)
                    def _():
                        acc_s[j, hf] = o
                        st_s[j, hf] = stat[j, hf]
                        o_up(j, hf).start()
                        s_up(j, hf).start()

    w_copy.wait()
    attq[...] = att[...].reshape(heads * HEAD_DIM, rows).T
    wide = pbuf.shape[2]
    piece_rows = pbuf.shape[1]
    chunks = keep.shape[0]

    def to_mate(n):
        return remote(send1.at[n], recv1.at[n], e1s.at[n], e1r.at[n], mate)

    def to_across(n):
        return remote(send2.at[n], recv2.at[n], e2s.at[n], e2r.at[n], across)

    def span(n):
        return pl.ds(pl.multiple_of(n * wide, wide), wide)

    @pl.loop(0, chunks + 1)
    def _(step):
        @pl.when(step < chunks)
        def _():
            n = step
            full = jnp.dot(attq[...], wbuf[:, span(n)], preferred_element_type=jnp.float32)
            pbuf[...] = full.reshape(4, piece_rows, wide)
            for t in range(2):
                send1[n, t] = pbuf[2 * t + 1 - core].astype(jnp.bfloat16)
                keep[n, t] = pbuf[2 * t + core]
            to_mate(n).start()

        @pl.when(step > 0)
        def _():
            n = step - 1
            to_mate(n).wait_recv()
            far = keep[n, 1 - a] + recv1[n, 1 - a].astype(jnp.float32)
            send2[n] = far.astype(jnp.bfloat16)
            to_across(n).start()

    @pl.loop(0, chunks)
    def _(n):
        to_across(n).wait_recv()
        near = keep[n, a] + recv1[n, a].astype(jnp.float32) + recv2[n].astype(jnp.float32)
        out_ref[:, span(n)] = near.astype(out_ref.dtype)

    @pl.loop(0, chunks)
    def _(n):
        to_mate(n).wait_send()
        to_across(n).wait_send()

    @pl.loop(0, heads)
    def _(h):
        k_side(h).wait_send()
        v_side(h).wait_send()

        @pl.when(below(0))
        def _():
            q_own(h).wait_send()

        @pl.when(gives)
        def _():
            k_look(h).wait_send()
            v_look(h).wait_send()

        @pl.loop(1, depth)
        def _(j):
            @pl.when(valid(j))
            def _():
                o_up(j, h).wait_send()
                s_up(j, h).wait_send()

                @pl.when(below(j))
                def _():
                    q_pass(j, h).wait_send()


def solution(mesh):
    n_ctx, n_tp = mesh.shape["ctx"], mesh.shape["tp"]

    def per_device(queries, keys, values, doc_ids, span_start, span_end, out_weight):
        rows, width = queries.shape
        heads = width // HEAD_DIM
        blocks = doc_ids.shape[0]
        nb = rows // BLOCK
        longest = blocks * 5 // 8
        reach = min(-(-(longest - 1) // nb), n_ctx - 1)
        levels = n_ctx // 2
        depth = min((reach + 1) // 2, levels - 1) + 1
        model = out_weight.shape[1]
        chunks = TAIL
        wide = model // chunks
        piece = rows // n_tp
        bf, f32, i32 = jnp.bfloat16, jnp.float32, jnp.int32
        dma = pltpu.SemaphoreType.DMA
        look = 3 * BLOCK
        smem = pl.BlockSpec(memory_space=pltpu.SMEM)
        anym = pl.BlockSpec(memory_space=pl.ANY)
        flops = 4 * rows * rows * 2 * width * depth + 2 * rows * width * model
        return pl.pallas_call(
            functools.partial(kernel, levels, reach),
            out_shape=jax.ShapeDtypeStruct((piece, model), bf),
            in_specs=[smem, smem, smem, anym, anym, anym, anym],
            out_specs=pl.BlockSpec(memory_space=pltpu.VMEM),
            scratch_shapes=[
                pltpu.VMEM((depth, heads, rows, HEAD_DIM), bf),
                pltpu.VMEM((heads, 2 * rows, HEAD_DIM), bf),
                pltpu.VMEM((heads, 2 * rows, HEAD_DIM), bf),
                pltpu.VMEM((heads, look, HEAD_DIM), bf),
                pltpu.VMEM((heads, look, HEAD_DIM), bf),
                pltpu.VMEM((depth, 2 * nb, 1, rows), i32),
                pltpu.VMEM((3, 1, rows), i32),
                pltpu.VMEM((depth, heads, HEAD_DIM, rows), f32),
                pltpu.VMEM((depth, heads, 8, rows), f32),
                pltpu.VMEM((depth, heads, HEAD_DIM, rows), bf),
                pltpu.VMEM((depth, heads, HEAD_DIM, rows), bf),
                pltpu.VMEM((depth, heads, 8, rows), f32),
                pltpu.VMEM((depth, heads, 8, rows), f32),
                pltpu.VMEM((heads, HEAD_DIM, rows), bf),
                pltpu.VMEM((rows, width), bf),
                pltpu.VMEM(out_weight.shape, bf),
                pltpu.VMEM((4, piece, wide), f32),
                pltpu.VMEM((chunks, 2, piece, wide), f32),
                pltpu.VMEM((chunks, 2, piece, wide), bf),
                pltpu.VMEM((chunks, 2, piece, wide), bf),
                pltpu.VMEM((chunks, piece, wide), bf),
                pltpu.VMEM((chunks, piece, wide), bf),
                pltpu.VMEM((2 * nb, BLOCK, rows), f32),
                pltpu.VMEM((2 * rows, rows), bf),
                pltpu.VMEM((HEAD_DIM, 2 * rows), bf),
                dma((depth, heads)), dma((depth, heads)),
                dma((2, heads)), dma((2, heads)),
                dma((2, heads)), dma((2, heads)),
                dma((depth, heads)), dma((depth, heads)),
                dma((depth, heads)), dma((depth, heads)),
                dma((3, heads)), dma,
                dma((chunks,)), dma((chunks,)),
                dma((chunks,)), dma((chunks,)),
            ],
            compiler_params=pltpu.CompilerParams(
                collective_id=0, has_side_effects=True, vmem_limit_bytes=60 * 1024 * 1024
            ),
            cost_estimate=pl.CostEstimate(
                flops=flops, bytes_accessed=8 * 1024 * 1024, transcendentals=0
            ),
        )(doc_ids, span_start, span_end, queries, keys, values, out_weight)

    return jax.shard_map(
        per_device,
        mesh=mesh,
        in_specs=(P("ctx", "tp"), P("ctx", "tp"), P("ctx", "tp"), P(), P(), P(), P("tp", None)),
        out_specs=P(("ctx", "tp"), None),
        check_vma=False,
    )
```

```python
import functools
import math

import jax
import jax.numpy as jnp
from jax import lax
from jax.experimental import pallas as pl
from jax.experimental.pallas import tpu as pltpu
from jax.sharding import PartitionSpec as P

HEAD_DIM = 128
BLOCK = 128
NEG = -1e30
FLOOR = -1e29
MESH = pl.DeviceIdType.MESH
TAIL = 8


def kernel(
    levels, reach, doc_ref, start_ref, end_ref, q_ref, k_ref, v_ref, w_ref, out_ref,
    qbuf, kbuf, vbuf, kla, vla, lim, limla, part, stat, acc_s, acc_r, st_s, st_r, att, attq,
    wbuf, pbuf, keep, send1, recv1, send2, recv2, sbuf, wts, vt,
    bar_q_s, q_r, kv_s, kv_r, la_s, la_r, o_s, o_r, s_s, s_r, loc, wsem, e1s, e1r, e2s, e2r,
):
    heads = qbuf.shape[1]
    rows = qbuf.shape[2]
    nb = rows // BLOCK
    depth = qbuf.shape[0]
    nspan = start_ref.shape[0]
    me = lax.axis_index("ctx")
    tp = lax.axis_index("tp")
    r, c = me // 2, me % 2
    a, core = tp // 2, tp % 2
    most = (reach + 1 - c) // 2
    const = math.log2(math.e) / math.sqrt(HEAD_DIM)

    up, down, side = (me + 2, tp), (me - 2, tp), (me + 1 - 2 * c, tp)
    mate, across = (me, tp + 1 - 2 * core), (me, tp + 2 - 4 * a)
    has_up, has_down = r < levels - 1, r > 0
    gives = (c == 0) & (r > 0)
    takes = (c == 1) & (r < levels - 1)

    barrier = pltpu.get_barrier_semaphore()
    for other in (side, mate, across):
        pl.semaphore_signal(barrier, inc=1, device_id=other, device_id_type=MESH)
    for cond, other in ((has_up, up), (has_down, down), (gives, (me - 1, tp)), (takes, (me + 1, tp))):
        @pl.when(cond)
        def _(other=other):
            pl.semaphore_signal(barrier, inc=1, device_id=other, device_id_type=MESH)

    w_copy = pltpu.make_async_copy(w_ref, wbuf, wsem)

    def cols(h):
        return pl.ds(pl.multiple_of(h * HEAD_DIM, HEAD_DIM), HEAD_DIM)

    mine = pl.ds(pl.multiple_of(c * rows, rows), rows)
    look = kla.shape[1]

    def local(j, h):
        src = (q_ref.at[:, cols(h)], k_ref.at[:, cols(h)], v_ref.at[:, cols(h)])[j]
        dst = (qbuf.at[0, h], kbuf.at[h, mine], vbuf.at[h, mine])[j]
        return pltpu.make_async_copy(src, dst, loc.at[j, h])

    def remote(src, dst, ss, rs, dev):
        return pltpu.make_async_remote_copy(
            src_ref=src, dst_ref=dst, send_sem=ss, recv_sem=rs, device_id=dev, device_id_type=MESH
        )

    def k_side(h):
        return remote(k_ref.at[:, cols(h)], kbuf.at[h, mine], kv_s.at[0, h], kv_r.at[0, h], side)

    def v_side(h):
        return remote(v_ref.at[:, cols(h)], vbuf.at[h, mine], kv_s.at[1, h], kv_r.at[1, h], side)

    def k_look(h):
        return remote(
            k_ref.at[pl.ds(0, look), cols(h)], kla.at[h], la_s.at[0, h], la_r.at[0, h], (me - 1, tp)
        )

    def v_look(h):
        return remote(
            v_ref.at[pl.ds(0, look), cols(h)], vla.at[h], la_s.at[1, h], la_r.at[1, h], (me - 1, tp)
        )

    def q_own(h):
        return remote(q_ref.at[:, cols(h)], qbuf.at[1, h], bar_q_s.at[0, h], q_r.at[1, h], down)

    def q_pass(j, h):
        return remote(qbuf.at[j, h], qbuf.at[j + 1, h], bar_q_s.at[j, h], q_r.at[j + 1, h], down)

    def o_up(j, h):
        return remote(acc_s.at[j, h], acc_r.at[j - 1, h], o_s.at[j, h], o_r.at[j - 1, h], up)

    def s_up(j, h):
        return remote(st_s.at[j, h], st_r.at[j - 1, h], s_s.at[j, h], s_r.at[j - 1, h], up)

    def valid(j):
        return (r + j < levels) & (j <= most)

    def below(j):
        return has_down & (j + 1 <= most)

    @pl.loop(0, heads)
    def _(h):
        for j in range(3):
            local(j, h).start()

    w_copy.start()
    total = 3 + sum(x.astype(jnp.int32) for x in (has_up, has_down, gives, takes))
    pl.semaphore_wait(barrier, total)

    @pl.loop(0, heads)
    def _(h):
        k_side(h).start()

        v_side(h).start()

    def give_own(h):
        @pl.when(below(0))
        def _():
            q_own(h).start()

        @pl.when(gives)
        def _():
            k_look(h).start()
            v_look(h).start()

    def pass_on(h):
        @pl.loop(1, depth)
        def _(j):
            @pl.when(valid(j))
            def _():
                remote(qbuf.at[j, h], qbuf.at[j, h], bar_q_s.at[j, h], q_r.at[j, h], up).wait_recv()

                @pl.when(below(j))
                def _():
                    q_pass(j, h).start()

    for h in range(min(2, heads)):
        give_own(h)

    def span_of(b):
        total = jnp.int32(-1)
        for s in range(nspan):
            total = jnp.where((b >= start_ref[s]) & (b < end_ref[s]), jnp.int32(s), total)
        return total

    lane = lax.broadcasted_iota(jnp.int32, (1, rows), 1)

    def row_of(values):
        row = jnp.full((1, rows), values[0], jnp.int32)
        for n in range(1, nb):
            row = jnp.where(lane >= n * BLOCK, values[n], row)
        return row

    def limit(qdoc, qspan, qpos, kb):
        kd, ks = doc_ref[kb], span_of(kb)
        reachable = jnp.where((qspan == ks) & (qspan >= 0), BLOCK, qpos - kb * BLOCK)
        return jnp.where(qdoc == kd, reachable, -1)

    @pl.loop(0, depth)
    def _(j):
        @pl.when(valid(j))
        def _():
            qi = me + 2 * j
            qdoc = row_of([doc_ref[qi * nb + n] for n in range(nb)])
            qspan = row_of([span_of(qi * nb + n) for n in range(nb)])
            qpos = lane + qi * rows
            for n in range(2 * nb):
                lim[j, n] = limit(qdoc, qspan, qpos, 2 * r * nb + n)

            @pl.when((j == 0) & takes)
            def _():
                for n in range(look // BLOCK):
                    limla[n] = limit(qdoc, qspan, qpos, (me + 1) * nb + n)

    half = rows // 2

    def piece(j, h, k_at, vt_at, lim_at, count):
        for side_q in range(2):
            lanes = slice(side_q * half, (side_q + 1) * half)
            q = qbuf[j, h, lanes, :]
            top = None
            for n in range(count):
                s = lax.dot_general(
                    k_at(n), q, (((1,), (1,)), ((), ())), preferred_element_type=jnp.float32
                )
                place = lax.broadcasted_iota(jnp.int32, (BLOCK, half), 0)
                s = jnp.where(place <= lim_at(n, lanes), s, NEG)
                sbuf[n, :, lanes] = s
                most_here = jnp.max(s.reshape(BLOCK // 8, 8, half), axis=0)
                top = most_here if top is None else jnp.maximum(top, most_here)
            m = jnp.maximum(jnp.max(top, axis=0, keepdims=True), FLOOR)
            shift = m * const
            total = jnp.zeros((8, half), jnp.float32)
            for n in range(count):
                p = jnp.exp2(sbuf[n, :, lanes] * const - shift)
                total = total + jnp.sum(p.reshape(BLOCK // 8, 8, half), axis=0)
                wts[n * BLOCK : (n + 1) * BLOCK, lanes] = p.astype(jnp.bfloat16)
            l = jnp.sum(total, axis=0, keepdims=True)
            o = jnp.dot(vt_at(), wts[: count * BLOCK, lanes], preferred_element_type=jnp.float32)
            yield lanes, o, m, l

    def merge(j, h, lanes, o, m, l, scale_o):
        om, ol = stat[j, h, 0:1, lanes], stat[j, h, 1:2, lanes]
        top = jnp.maximum(m, om)
        f_new = jnp.exp2((m - top) * const)
        f_old = jnp.exp2((om - top) * const)
        part[j, h, :, lanes] = part[j, h, :, lanes] * f_old + o * (f_new * scale_o)
        stat[j, h, 0:1, lanes] = top
        stat[j, h, 1:2, lanes] = ol * f_old + l * f_new

    def put(j, h, results):
        for lanes, o, m, l in results:
            part[j, h, :, lanes] = o
            stat[j, h, 0:1, lanes] = m
            stat[j, h, 1:2, lanes] = l

    lag = 2
    pass_on(0)

    @pl.loop(0, heads + lag)
    def _(step):
        @pl.when(step < heads)
        def _():
            h = step

            for j in range(3):
                local(j, h).wait()
            k_side(h).wait_recv()
            v_side(h).wait_recv()

            vt[...] = vbuf[h].T

            @pl.loop(0, depth)
            def _(j):
                far = 2 * j + c > reach

                def block(first):
                    return lambda n: kbuf[h, (first + n) * BLOCK : (first + n + 1) * BLOCK, :]

                @pl.when(valid(j) & jnp.logical_not(far))
                def _():
                    put(j, h, piece(
                        j, h, block(0), lambda: vt[...], lambda n, lanes: lim[j, n, :, lanes], 2 * nb
                    ))

                @pl.when(valid(j) & far)
                def _():
                    put(j, h, piece(
                        j, h, block(nb), lambda: vt[:, rows:],
                        lambda n, lanes: lim[j, nb + n, :, lanes], nb
                    ))

        @pl.when(step + 2 < heads)
        def _():
            give_own(step + 2)

        @pl.when(step + 1 < heads)
        def _():
            pass_on(step + 1)

        hf = jnp.where(has_down, step - lag, step)

        @pl.when((hf >= 0) & (hf < heads))
        def _():
            @pl.when(takes)
            def _():
                k_look(hf).wait_recv()
                v_look(hf).wait_recv()
                vt[:, :look] = vla[hf].T
                for lanes, o, m, l in piece(
                    0, hf, lambda n: kla[hf, n * BLOCK : (n + 1) * BLOCK, :], lambda: vt[:, :look],
                    lambda n, lanes: limla[n, :, lanes], look // BLOCK
                ):
                    merge(0, hf, lanes, o, m, l, 1.0)

            @pl.loop(0, depth)
            def _(j):
                @pl.when(valid(j))
                def _():
                    @pl.when(below(j))
                    def _():
                        remote(acc_s.at[j, hf], acc_r.at[j, hf], o_s.at[j, hf], o_r.at[j, hf], down).wait_recv()
                        remote(st_s.at[j, hf], st_r.at[j, hf], s_s.at[j, hf], s_r.at[j, hf], down).wait_recv()
                        m, l = st_r[j, hf, 0:1], st_r[j, hf, 1:2]
                        merge(j, hf, slice(None), acc_r[j, hf].astype(jnp.float32), m, l, l)

                    l = stat[j, hf, 1:2]
                    o = (part[j, hf] * (1.0 / jnp.where(l > 0.0, l, 1.0))).astype(jnp.bfloat16)

                    @pl.when(j == 0)
                    def _():
                        att[hf] = o

                    @pl.when(j > 0)
                    def _():
                        acc_s[j, hf] = o
                        st_s[j, hf] = stat[j, hf]
                        o_up(j, hf).start()
                        s_up(j, hf).start()

    w_copy.wait()
    attq[...] = att[...].reshape(heads * HEAD_DIM, rows).T
    wide = pbuf.shape[2]
    piece_rows = pbuf.shape[1]
    chunks = keep.shape[0]

    def to_mate(n):
        return remote(send1.at[n], recv1.at[n], e1s.at[n], e1r.at[n], mate)

    def to_across(n):
        return remote(send2.at[n], recv2.at[n], e2s.at[n], e2r.at[n], across)

    def span(n):
        return pl.ds(pl.multiple_of(n * wide, wide), wide)

    @pl.loop(0, chunks + 1)
    def _(step):
        @pl.when(step < chunks)
        def _():
            n = step
            full = jnp.dot(attq[...], wbuf[:, span(n)], preferred_element_type=jnp.float32)
            pbuf[...] = full.reshape(4, piece_rows, wide)
            for t in range(2):
                send1[n, t] = pbuf[2 * t + 1 - core].astype(jnp.bfloat16)
                keep[n, t] = pbuf[2 * t + core]
            to_mate(n).start()

        @pl.when(step > 0)
        def _():
            n = step - 1
            to_mate(n).wait_recv()
            far = keep[n, 1 - a] + recv1[n, 1 - a].astype(jnp.float32)
            send2[n] = far.astype(jnp.bfloat16)
            to_across(n).start()

    @pl.loop(0, chunks)
    def _(n):
        to_across(n).wait_recv()
        near = keep[n, a] + recv1[n, a].astype(jnp.float32) + recv2[n].astype(jnp.float32)
        out_ref[:, span(n)] = near.astype(out_ref.dtype)

    @pl.loop(0, chunks)
    def _(n):
        to_mate(n).wait_send()
        to_across(n).wait_send()

    @pl.loop(0, heads)
    def _(h):
        k_side(h).wait_send()
        v_side(h).wait_send()

        @pl.when(below(0))
        def _():
            q_own(h).wait_send()

        @pl.when(gives)
        def _():
            k_look(h).wait_send()
            v_look(h).wait_send()

        @pl.loop(1, depth)
        def _(j):
            @pl.when(valid(j))
            def _():
                o_up(j, h).wait_send()
                s_up(j, h).wait_send()

                @pl.when(below(j))
                def _():
                    q_pass(j, h).wait_send()


def solution(mesh):
    n_ctx, n_tp = mesh.shape["ctx"], mesh.shape["tp"]

    def per_device(queries, keys, values, doc_ids, span_start, span_end, out_weight):
        rows, width = queries.shape
        heads = width // HEAD_DIM
        blocks = doc_ids.shape[0]
        nb = rows // BLOCK
        longest = blocks * 5 // 8
        reach = min(-(-(longest - 1) // nb), n_ctx - 1)
        levels = n_ctx // 2
        depth = min((reach + 1) // 2, levels - 1) + 1
        model = out_weight.shape[1]
        chunks = TAIL
        wide = model // chunks
        piece = rows // n_tp
        bf, f32, i32 = jnp.bfloat16, jnp.float32, jnp.int32
        dma = pltpu.SemaphoreType.DMA
        look = 3 * BLOCK
        smem = pl.BlockSpec(memory_space=pltpu.SMEM)
        anym = pl.BlockSpec(memory_space=pl.ANY)
        flops = 4 * rows * rows * 2 * width * depth + 2 * rows * width * model
        return pl.pallas_call(
            functools.partial(kernel, levels, reach),
            out_shape=jax.ShapeDtypeStruct((piece, model), bf),
            in_specs=[smem, smem, smem, anym, anym, anym, anym],
            out_specs=pl.BlockSpec(memory_space=pltpu.VMEM),
            scratch_shapes=[
                pltpu.VMEM((depth, heads, rows, HEAD_DIM), bf),
                pltpu.VMEM((heads, 2 * rows, HEAD_DIM), bf),
                pltpu.VMEM((heads, 2 * rows, HEAD_DIM), bf),
                pltpu.VMEM((heads, look, HEAD_DIM), bf),
                pltpu.VMEM((heads, look, HEAD_DIM), bf),
                pltpu.VMEM((depth, 2 * nb, 1, rows), i32),
                pltpu.VMEM((3, 1, rows), i32),
                pltpu.VMEM((depth, heads, HEAD_DIM, rows), f32),
                pltpu.VMEM((depth, heads, 8, rows), f32),
                pltpu.VMEM((depth, heads, HEAD_DIM, rows), bf),
                pltpu.VMEM((depth, heads, HEAD_DIM, rows), bf),
                pltpu.VMEM((depth, heads, 8, rows), f32),
                pltpu.VMEM((depth, heads, 8, rows), f32),
                pltpu.VMEM((heads, HEAD_DIM, rows), bf),
                pltpu.VMEM((rows, width), bf),
                pltpu.VMEM(out_weight.shape, bf),
                pltpu.VMEM((4, piece, wide), f32),
                pltpu.VMEM((chunks, 2, piece, wide), f32),
                pltpu.VMEM((chunks, 2, piece, wide), bf),
                pltpu.VMEM((chunks, 2, piece, wide), bf),
                pltpu.VMEM((chunks, piece, wide), bf),
                pltpu.VMEM((chunks, piece, wide), bf),
                pltpu.VMEM((2 * nb, BLOCK, rows), f32),
                pltpu.VMEM((2 * rows, rows), bf),
                pltpu.VMEM((HEAD_DIM, 2 * rows), bf),
                dma((depth, heads)), dma((depth, heads)),
                dma((2, heads)), dma((2, heads)),
                dma((2, heads)), dma((2, heads)),
                dma((depth, heads)), dma((depth, heads)),
                dma((depth, heads)), dma((depth, heads)),
                dma((3, heads)), dma,
                dma((chunks,)), dma((chunks,)),
                dma((chunks,)), dma((chunks,)),
            ],
            compiler_params=pltpu.CompilerParams(
                collective_id=0, has_side_effects=True, vmem_limit_bytes=60 * 1024 * 1024
            ),
            cost_estimate=pl.CostEstimate(
                flops=flops, bytes_accessed=8 * 1024 * 1024, transcendentals=0
            ),
        )(doc_ids, span_start, span_end, queries, keys, values, out_weight)

    return jax.shard_map(
        per_device,
        mesh=mesh,
        in_specs=(P("ctx", "tp"), P("ctx", "tp"), P("ctx", "tp"), P(), P(), P(), P("tp", None)),
        out_specs=P(("ctx", "tp"), None),
        check_vma=False,
    )
```

```python
import functools
import math

import jax
import jax.numpy as jnp
from jax import lax
from jax.experimental import pallas as pl
from jax.experimental.pallas import tpu as pltpu
from jax.sharding import PartitionSpec as P

HEAD_DIM = 128
BLOCK = 128
NEG = -1e30
FLOOR = -1e29
MESH = pl.DeviceIdType.MESH
TAIL = 8


def kernel(
    levels, reach, ahead, doc_ref, start_ref, end_ref, q_ref, k_ref, v_ref, w_ref, out_ref,
    qbuf, kbuf, vbuf, kla, vla, lim, limla, part, stat, acc_s, acc_r, st_s, st_r, att, attq,
    wbuf, pbuf, keep, send1, recv1, send2, recv2, sbuf, wts, vt,
    bar_q_s, q_r, kv_s, kv_r, la_s, la_r, o_s, o_r, s_s, s_r, loc, wsem, e1s, e1r, e2s, e2r,
):
    heads = qbuf.shape[1]
    rows = qbuf.shape[2]
    nb = rows // BLOCK
    depth = qbuf.shape[0]
    nspan = start_ref.shape[0]
    me = lax.axis_index("ctx")
    tp = lax.axis_index("tp")
    r, c = me // 2, me % 2
    a, core = tp // 2, tp % 2
    most = jnp.minimum((reach + 1 - c) // 2, depth - 1)
    const = math.log2(math.e) / math.sqrt(HEAD_DIM)

    up, down, side = (me + 2, tp), (me - 2, tp), (me + 1 - 2 * c, tp)
    mate, across = (me, tp + 1 - 2 * core), (me, tp + 2 - 4 * a)
    has_up, has_down = r < levels - 1, r > 0
    gives = (c == 0) & (r > 0)
    takes = (c == 1) & (r < levels - 1)
    greeted = ((has_up, up), (has_down, down))
    if ahead:
        greeted += ((gives, (me - 1, tp)), (takes, (me + 1, tp)))

    barrier = pltpu.get_barrier_semaphore()
    for other in (side, mate, across):
        pl.semaphore_signal(barrier, inc=1, device_id=other, device_id_type=MESH)
    for cond, other in greeted:
        @pl.when(cond)
        def _(other=other):
            pl.semaphore_signal(barrier, inc=1, device_id=other, device_id_type=MESH)

    w_copy = pltpu.make_async_copy(w_ref, wbuf, wsem)

    def cols(h):
        return pl.ds(pl.multiple_of(h * HEAD_DIM, HEAD_DIM), HEAD_DIM)

    mine = pl.ds(pl.multiple_of(c * rows, rows), rows)
    look = kla.shape[1]

    def local(j, h):
        src = (q_ref.at[:, cols(h)], k_ref.at[:, cols(h)], v_ref.at[:, cols(h)])[j]
        dst = (qbuf.at[0, h], kbuf.at[h, mine], vbuf.at[h, mine])[j]
        return pltpu.make_async_copy(src, dst, loc.at[j, h])

    def remote(src, dst, ss, rs, dev):
        return pltpu.make_async_remote_copy(
            src_ref=src, dst_ref=dst, send_sem=ss, recv_sem=rs, device_id=dev, device_id_type=MESH
        )

    def k_side(h):
        return remote(k_ref.at[:, cols(h)], kbuf.at[h, mine], kv_s.at[0, h], kv_r.at[0, h], side)

    def v_side(h):
        return remote(v_ref.at[:, cols(h)], vbuf.at[h, mine], kv_s.at[1, h], kv_r.at[1, h], side)

    def k_look(h):
        return remote(
            k_ref.at[pl.ds(0, look), cols(h)], kla.at[h], la_s.at[0, h], la_r.at[0, h], (me - 1, tp)
        )

    def v_look(h):
        return remote(
            v_ref.at[pl.ds(0, look), cols(h)], vla.at[h], la_s.at[1, h], la_r.at[1, h], (me - 1, tp)
        )

    def q_own(h):
        return remote(q_ref.at[:, cols(h)], qbuf.at[1, h], bar_q_s.at[0, h], q_r.at[1, h], down)

    def q_pass(j, h):
        return remote(qbuf.at[j, h], qbuf.at[j + 1, h], bar_q_s.at[j, h], q_r.at[j + 1, h], down)

    def o_up(j, h):
        return remote(acc_s.at[j, h], acc_r.at[j - 1, h], o_s.at[j, h], o_r.at[j - 1, h], up)

    def s_up(j, h):
        return remote(st_s.at[j, h], st_r.at[j - 1, h], s_s.at[j, h], s_r.at[j - 1, h], up)

    def valid(j):
        return (r + j < levels) & (j <= most)

    def below(j):
        return has_down & (j + 1 <= most)

    @pl.loop(0, heads)
    def _(h):
        for j in range(3):
            local(j, h).start()

    w_copy.start()
    total = 3 + sum(x.astype(jnp.int32) for x, _ in greeted)
    pl.semaphore_wait(barrier, total)

    @pl.loop(0, heads)
    def _(h):
        k_side(h).start()

        v_side(h).start()

    def give_own(h):
        @pl.when(below(0))
        def _():
            q_own(h).start()

        if ahead:

            @pl.when(gives)
            def _():
                k_look(h).start()
                v_look(h).start()

    def pass_on(h):
        @pl.loop(1, depth)
        def _(j):
            @pl.when(valid(j))
            def _():
                remote(qbuf.at[j, h], qbuf.at[j, h], bar_q_s.at[j, h], q_r.at[j, h], up).wait_recv()

                @pl.when(below(j))
                def _():
                    q_pass(j, h).start()

    for h in range(min(2, heads)):
        give_own(h)

    def span_of(b):
        total = jnp.int32(-1)
        for s in range(nspan):
            total = jnp.where((b >= start_ref[s]) & (b < end_ref[s]), jnp.int32(s), total)
        return total

    lane = lax.broadcasted_iota(jnp.int32, (1, rows), 1)

    def row_of(values):
        row = jnp.full((1, rows), values[0], jnp.int32)
        for n in range(1, nb):
            row = jnp.where(lane >= n * BLOCK, values[n], row)
        return row

    def limit(qdoc, qspan, qpos, kb):
        kd, ks = doc_ref[kb], span_of(kb)
        reachable = jnp.where((qspan == ks) & (qspan >= 0), BLOCK, qpos - kb * BLOCK)
        return jnp.where(qdoc == kd, reachable, -1)

    @pl.loop(0, depth)
    def _(j):
        @pl.when(valid(j))
        def _():
            qi = me + 2 * j
            qdoc = row_of([doc_ref[qi * nb + n] for n in range(nb)])
            qspan = row_of([span_of(qi * nb + n) for n in range(nb)])
            qpos = lane + qi * rows
            for n in range(2 * nb):
                lim[j, n] = limit(qdoc, qspan, qpos, 2 * r * nb + n)

            if ahead:

                @pl.when((j == 0) & takes)
                def _():
                    for n in range(look // BLOCK):
                        limla[n] = limit(qdoc, qspan, qpos, (me + 1) * nb + n)

    half = rows // 2

    def piece(j, h, k_at, vt_at, lim_at, count):
        for side_q in range(2):
            lanes = slice(side_q * half, (side_q + 1) * half)
            q = qbuf[j, h, lanes, :]
            top = None
            for n in range(count):
                s = lax.dot_general(
                    k_at(n), q, (((1,), (1,)), ((), ())), preferred_element_type=jnp.float32
                )
                place = lax.broadcasted_iota(jnp.int32, (BLOCK, half), 0)
                s = jnp.where(place <= lim_at(n, lanes), s, NEG)
                sbuf[n, :, lanes] = s
                most_here = jnp.max(s.reshape(BLOCK // 8, 8, half), axis=0)
                top = most_here if top is None else jnp.maximum(top, most_here)
            m = jnp.maximum(jnp.max(top, axis=0, keepdims=True), FLOOR)
            shift = m * const
            total = jnp.zeros((8, half), jnp.float32)
            for n in range(count):
                p = jnp.exp2(sbuf[n, :, lanes] * const - shift)
                total = total + jnp.sum(p.reshape(BLOCK // 8, 8, half), axis=0)
                wts[n * BLOCK : (n + 1) * BLOCK, lanes] = p.astype(jnp.bfloat16)
            l = jnp.sum(total, axis=0, keepdims=True)
            o = jnp.dot(vt_at(), wts[: count * BLOCK, lanes], preferred_element_type=jnp.float32)
            yield lanes, o, m, l

    def merge(j, h, lanes, o, m, l, scale_o):
        om, ol = stat[j, h, 0:1, lanes], stat[j, h, 1:2, lanes]
        top = jnp.maximum(m, om)
        f_new = jnp.exp2((m - top) * const)
        f_old = jnp.exp2((om - top) * const)
        part[j, h, :, lanes] = part[j, h, :, lanes] * f_old + o * (f_new * scale_o)
        stat[j, h, 0:1, lanes] = top
        stat[j, h, 1:2, lanes] = ol * f_old + l * f_new

    def put(j, h, results):
        for lanes, o, m, l in results:
            part[j, h, :, lanes] = o
            stat[j, h, 0:1, lanes] = m
            stat[j, h, 1:2, lanes] = l

    lag = 2
    pass_on(0)

    @pl.loop(0, heads + lag)
    def _(step):
        @pl.when(step < heads)
        def _():
            h = step

            for j in range(3):
                local(j, h).wait()
            k_side(h).wait_recv()
            v_side(h).wait_recv()

            vt[...] = vbuf[h].T

            @pl.loop(0, depth)
            def _(j):
                far = 2 * j + c > reach

                def block(first):
                    return lambda n: kbuf[h, (first + n) * BLOCK : (first + n + 1) * BLOCK, :]

                @pl.when(valid(j) & jnp.logical_not(far))
                def _():
                    put(j, h, piece(
                        j, h, block(0), lambda: vt[...], lambda n, lanes: lim[j, n, :, lanes], 2 * nb
                    ))

                if 2 * depth - 1 > reach:

                    @pl.when(valid(j) & far)
                    def _():
                        put(j, h, piece(
                            j, h, block(nb), lambda: vt[:, rows:],
                            lambda n, lanes: lim[j, nb + n, :, lanes], nb
                        ))

        @pl.when(step + 2 < heads)
        def _():
            give_own(step + 2)

        @pl.when(step + 1 < heads)
        def _():
            pass_on(step + 1)

        hf = jnp.where(has_down, step - lag, step)

        @pl.when((hf >= 0) & (hf < heads))
        def _():
            if ahead:

                @pl.when(takes)
                def _():
                    k_look(hf).wait_recv()
                    v_look(hf).wait_recv()
                    vt[:, :look] = vla[hf].T
                    for lanes, o, m, l in piece(
                        0, hf, lambda n: kla[hf, n * BLOCK : (n + 1) * BLOCK, :], lambda: vt[:, :look],
                        lambda n, lanes: limla[n, :, lanes], look // BLOCK
                    ):
                        merge(0, hf, lanes, o, m, l, 1.0)

            @pl.loop(0, depth)
            def _(j):
                @pl.when(valid(j))
                def _():
                    @pl.when(below(j))
                    def _():
                        remote(acc_s.at[j, hf], acc_r.at[j, hf], o_s.at[j, hf], o_r.at[j, hf], down).wait_recv()
                        remote(st_s.at[j, hf], st_r.at[j, hf], s_s.at[j, hf], s_r.at[j, hf], down).wait_recv()
                        m, l = st_r[j, hf, 0:1], st_r[j, hf, 1:2]
                        merge(j, hf, slice(None), acc_r[j, hf].astype(jnp.float32), m, l, l)

                    l = stat[j, hf, 1:2]
                    o = (part[j, hf] * (1.0 / jnp.where(l > 0.0, l, 1.0))).astype(jnp.bfloat16)

                    @pl.when(j == 0)
                    def _():
                        att[hf] = o

                    @pl.when(j > 0)
                    def _():
                        acc_s[j, hf] = o
                        st_s[j, hf] = stat[j, hf]
                        o_up(j, hf).start()
                        s_up(j, hf).start()

    w_copy.wait()
    attq[...] = att[...].reshape(heads * HEAD_DIM, rows).T
    wide = pbuf.shape[2]
    piece_rows = pbuf.shape[1]
    chunks = keep.shape[0]

    def to_mate(n):
        return remote(send1.at[n], recv1.at[n], e1s.at[n], e1r.at[n], mate)

    def to_across(n):
        return remote(send2.at[n], recv2.at[n], e2s.at[n], e2r.at[n], across)

    def span(n):
        return pl.ds(pl.multiple_of(n * wide, wide), wide)

    @pl.loop(0, chunks + 1)
    def _(step):
        @pl.when(step < chunks)
        def _():
            n = step
            full = jnp.dot(attq[...], wbuf[:, span(n)], preferred_element_type=jnp.float32)
            pbuf[...] = full.reshape(4, piece_rows, wide)
            for t in range(2):
                send1[n, t] = pbuf[2 * t + 1 - core].astype(jnp.bfloat16)
                keep[n, t] = pbuf[2 * t + core]
            to_mate(n).start()

        @pl.when(step > 0)
        def _():
            n = step - 1
            to_mate(n).wait_recv()
            far = keep[n, 1 - a] + recv1[n, 1 - a].astype(jnp.float32)
            send2[n] = far.astype(jnp.bfloat16)
            to_across(n).start()

    @pl.loop(0, chunks)
    def _(n):
        to_across(n).wait_recv()
        near = keep[n, a] + recv1[n, a].astype(jnp.float32) + recv2[n].astype(jnp.float32)
        out_ref[:, span(n)] = near.astype(out_ref.dtype)

    @pl.loop(0, chunks)
    def _(n):
        to_mate(n).wait_send()
        to_across(n).wait_send()

    @pl.loop(0, heads)
    def _(h):
        k_side(h).wait_send()
        v_side(h).wait_send()

        @pl.when(below(0))
        def _():
            q_own(h).wait_send()

        if ahead:

            @pl.when(gives)
            def _():
                k_look(h).wait_send()
                v_look(h).wait_send()

        @pl.loop(1, depth)
        def _(j):
            @pl.when(valid(j))
            def _():
                o_up(j, h).wait_send()
                s_up(j, h).wait_send()

                @pl.when(below(j))
                def _():
                    q_pass(j, h).wait_send()


def solution(mesh):
    n_ctx, n_tp = mesh.shape["ctx"], mesh.shape["tp"]

    def per_device(queries, keys, values, doc_ids, span_start, span_end, out_weight):
        rows, width = queries.shape
        heads = width // HEAD_DIM
        blocks = doc_ids.shape[0]
        nb = rows // BLOCK
        longest = blocks * 5 // 8
        reach = min(-(-(longest - 1) // nb), n_ctx - 1)
        levels = n_ctx // 2
        depth = min((reach + 1) // 2, levels - 1) + 1
        model = out_weight.shape[1]
        chunks = TAIL
        wide = model // chunks
        piece = rows // n_tp
        bf, f32, i32 = jnp.bfloat16, jnp.float32, jnp.int32
        dma = pltpu.SemaphoreType.DMA
        look = 3 * BLOCK
        smem = pl.BlockSpec(memory_space=pltpu.SMEM)
        anym = pl.BlockSpec(memory_space=pl.ANY)
        flops = 4 * rows * rows * 2 * width * depth + 2 * rows * width * model
        def attend(depth, ahead, ident):
            return pl.pallas_call(
                functools.partial(kernel, levels, reach, ahead),
                out_shape=jax.ShapeDtypeStruct((piece, model), bf),
                in_specs=[smem, smem, smem, anym, anym, anym, anym],
                out_specs=pl.BlockSpec(memory_space=pltpu.VMEM),
                scratch_shapes=[
                    pltpu.VMEM((depth, heads, rows, HEAD_DIM), bf),
                    pltpu.VMEM((heads, 2 * rows, HEAD_DIM), bf),
                    pltpu.VMEM((heads, 2 * rows, HEAD_DIM), bf),
                    pltpu.VMEM((heads, look, HEAD_DIM), bf),
                    pltpu.VMEM((heads, look, HEAD_DIM), bf),
                    pltpu.VMEM((depth, 2 * nb, 1, rows), i32),
                    pltpu.VMEM((3, 1, rows), i32),
                    pltpu.VMEM((depth, heads, HEAD_DIM, rows), f32),
                    pltpu.VMEM((depth, heads, 8, rows), f32),
                    pltpu.VMEM((depth, heads, HEAD_DIM, rows), bf),
                    pltpu.VMEM((depth, heads, HEAD_DIM, rows), bf),
                    pltpu.VMEM((depth, heads, 8, rows), f32),
                    pltpu.VMEM((depth, heads, 8, rows), f32),
                    pltpu.VMEM((heads, HEAD_DIM, rows), bf),
                    pltpu.VMEM((rows, width), bf),
                    pltpu.VMEM(out_weight.shape, bf),
                    pltpu.VMEM((4, piece, wide), f32),
                    pltpu.VMEM((chunks, 2, piece, wide), f32),
                    pltpu.VMEM((chunks, 2, piece, wide), bf),
                    pltpu.VMEM((chunks, 2, piece, wide), bf),
                    pltpu.VMEM((chunks, piece, wide), bf),
                    pltpu.VMEM((chunks, piece, wide), bf),
                    pltpu.VMEM((2 * nb, BLOCK, rows), f32),
                    pltpu.VMEM((2 * rows, rows), bf),
                    pltpu.VMEM((HEAD_DIM, 2 * rows), bf),
                    dma((depth, heads)), dma((depth, heads)),
                    dma((2, heads)), dma((2, heads)),
                    dma((2, heads)), dma((2, heads)),
                    dma((depth, heads)), dma((depth, heads)),
                    dma((depth, heads)), dma((depth, heads)),
                    dma((3, heads)), dma,
                    dma((chunks,)), dma((chunks,)),
                    dma((chunks,)), dma((chunks,)),
                ],
                compiler_params=pltpu.CompilerParams(
                    collective_id=ident, has_side_effects=True, vmem_limit_bytes=60 * 1024 * 1024
                ),
                cost_estimate=pl.CostEstimate(
                    flops=flops, bytes_accessed=8 * 1024 * 1024, transcendentals=0
                ),
            )

        level = jnp.arange(blocks, dtype=jnp.int32) // (2 * nb)
        same = doc_ids[:, None] == doc_ids[None, :]
        farthest = jnp.max(jnp.where(same, level[:, None] - level[None, :], 0))
        crossing = jnp.any(span_start // (2 * nb) != (span_end - 1) // (2 * nb))
        which = jnp.where(crossing, 0, jnp.where(farthest < depth - 1, 2, 1))
        return lax.switch(
            which,
            [attend(depth, True, 0), attend(depth, False, 1), attend(max(depth - 1, 1), False, 2)],
            doc_ids, span_start, span_end, queries, keys, values, out_weight,
        )


    return jax.shard_map(
        per_device,
        mesh=mesh,
        in_specs=(P("ctx", "tp"), P("ctx", "tp"), P("ctx", "tp"), P(), P(), P(), P("tp", None)),
        out_specs=P(("ctx", "tp"), None),
        check_vma=False,
    )
```

```python
import functools
import math

import jax
import jax.numpy as jnp
from jax import lax
from jax.experimental import pallas as pl
from jax.experimental.pallas import tpu as pltpu
from jax.sharding import PartitionSpec as P

HEAD_DIM = 128
BLOCK = 128
NEG = -1e30
FLOOR = -1e29
MESH = pl.DeviceIdType.MESH
TAIL = 8


def kernel(
    levels, reach, ahead, doc_ref, start_ref, end_ref, q_ref, k_ref, v_ref, w_ref, out_ref,
    qbuf, kbuf, vbuf, kla, vla, lim, limla, part, stat, acc_s, acc_r, st_s, st_r, att, attq,
    wbuf, pbuf, keep, send1, recv1, send2, recv2, sbuf, wts, vt,
    bar_q_s, q_r, kv_s, kv_r, la_s, la_r, o_s, o_r, s_s, s_r, loc, wsem, e1s, e1r, e2s, e2r,
):
    heads = qbuf.shape[1]
    rows = qbuf.shape[2]
    nb = rows // BLOCK
    depth = qbuf.shape[0]
    nspan = start_ref.shape[0]
    me = lax.axis_index("ctx")
    tp = lax.axis_index("tp")
    r, c = me // 2, me % 2
    a, core = tp // 2, tp % 2
    most = jnp.minimum((reach + 1 - c) // 2, depth - 1)
    const = math.log2(math.e) / math.sqrt(HEAD_DIM)

    up, down, side = (me + 2, tp), (me - 2, tp), (me + 1 - 2 * c, tp)
    mate, across = (me, tp + 1 - 2 * core), (me, tp + 2 - 4 * a)
    has_up, has_down = r < levels - 1, r > 0
    gives = (c == 0) & (r > 0)
    takes = (c == 1) & (r < levels - 1)
    greeted = ((has_up, up), (has_down, down))
    if ahead:
        greeted += ((gives, (me - 1, tp)), (takes, (me + 1, tp)))

    barrier = pltpu.get_barrier_semaphore()
    for other in (side, mate, across):
        pl.semaphore_signal(barrier, inc=1, device_id=other, device_id_type=MESH)
    for cond, other in greeted:
        @pl.when(cond)
        def _(other=other):
            pl.semaphore_signal(barrier, inc=1, device_id=other, device_id_type=MESH)

    w_copy = pltpu.make_async_copy(w_ref, wbuf, wsem)

    def cols(h):
        return pl.ds(pl.multiple_of(h * HEAD_DIM, HEAD_DIM), HEAD_DIM)

    mine = pl.ds(pl.multiple_of(c * rows, rows), rows)
    look = kla.shape[1]

    def local(j, h):
        src = (q_ref.at[:, cols(h)], k_ref.at[:, cols(h)], v_ref.at[:, cols(h)])[j]
        dst = (qbuf.at[0, h], kbuf.at[h, mine], vbuf.at[h, mine])[j]
        return pltpu.make_async_copy(src, dst, loc.at[j, h])

    def remote(src, dst, ss, rs, dev):
        return pltpu.make_async_remote_copy(
            src_ref=src, dst_ref=dst, send_sem=ss, recv_sem=rs, device_id=dev, device_id_type=MESH
        )

    def k_side(h):
        return remote(k_ref.at[:, cols(h)], kbuf.at[h, mine], kv_s.at[0, h], kv_r.at[0, h], side)

    def v_side(h):
        return remote(v_ref.at[:, cols(h)], vbuf.at[h, mine], kv_s.at[1, h], kv_r.at[1, h], side)

    def k_look(h):
        return remote(
            k_ref.at[pl.ds(0, look), cols(h)], kla.at[h], la_s.at[0, h], la_r.at[0, h], (me - 1, tp)
        )

    def v_look(h):
        return remote(
            v_ref.at[pl.ds(0, look), cols(h)], vla.at[h], la_s.at[1, h], la_r.at[1, h], (me - 1, tp)
        )

    def q_own(h):
        return remote(q_ref.at[:, cols(h)], qbuf.at[1, h], bar_q_s.at[0, h], q_r.at[1, h], down)

    def q_pass(j, h):
        return remote(qbuf.at[j, h], qbuf.at[j + 1, h], bar_q_s.at[j, h], q_r.at[j + 1, h], down)

    def o_up(j, h):
        return remote(acc_s.at[j, h], acc_r.at[j - 1, h], o_s.at[j, h], o_r.at[j - 1, h], up)

    def s_up(j, h):
        return remote(st_s.at[j, h], st_r.at[j - 1, h], s_s.at[j, h], s_r.at[j - 1, h], up)

    def valid(j):
        return (r + j < levels) & (j <= most)

    def below(j):
        return has_down & (j + 1 <= most)

    @pl.loop(0, heads)
    def _(h):
        for j in range(3):
            local(j, h).start()

    w_copy.start()
    total = 3 + sum(x.astype(jnp.int32) for x, _ in greeted)
    pl.semaphore_wait(barrier, total)

    @pl.loop(0, heads)
    def _(h):
        k_side(h).start()

        v_side(h).start()

    def give_own(h):
        @pl.when(below(0))
        def _():
            q_own(h).start()

        if ahead:

            @pl.when(gives)
            def _():
                k_look(h).start()
                v_look(h).start()

    def pass_on(h):
        @pl.loop(1, depth)
        def _(j):
            @pl.when(valid(j))
            def _():
                remote(qbuf.at[j, h], qbuf.at[j, h], bar_q_s.at[j, h], q_r.at[j, h], up).wait_recv()

                @pl.when(below(j))
                def _():
                    q_pass(j, h).start()

    for h in range(min(2, heads)):
        give_own(h)

    def span_of(b):
        total = jnp.int32(-1)
        for s in range(nspan):
            total = jnp.where((b >= start_ref[s]) & (b < end_ref[s]), jnp.int32(s), total)
        return total

    lane = lax.broadcasted_iota(jnp.int32, (1, rows), 1)

    def row_of(values):
        row = jnp.full((1, rows), values[0], jnp.int32)
        for n in range(1, nb):
            row = jnp.where(lane >= n * BLOCK, values[n], row)
        return row

    def limit(qdoc, qspan, qpos, kb):
        kd, ks = doc_ref[kb], span_of(kb)
        reachable = jnp.where((qspan == ks) & (qspan >= 0), BLOCK, qpos - kb * BLOCK)
        return jnp.where(qdoc == kd, reachable, -1)

    @pl.loop(0, depth)
    def _(j):
        @pl.when(valid(j))
        def _():
            qi = me + 2 * j
            qdoc = row_of([doc_ref[qi * nb + n] for n in range(nb)])
            qspan = row_of([span_of(qi * nb + n) for n in range(nb)])
            qpos = lane + qi * rows
            for n in range(2 * nb):
                lim[j, n] = limit(qdoc, qspan, qpos, 2 * r * nb + n)

            if ahead:

                @pl.when((j == 0) & takes)
                def _():
                    for n in range(look // BLOCK):
                        limla[n] = limit(qdoc, qspan, qpos, (me + 1) * nb + n)

    half = rows // 2

    def piece(j, h, k_at, vt_at, lim_at, count):
        for side_q in range(2):
            lanes = slice(side_q * half, (side_q + 1) * half)
            q = qbuf[j, h, lanes, :]
            top = None
            for n in range(count):
                s = lax.dot_general(
                    k_at(n), q, (((1,), (1,)), ((), ())), preferred_element_type=jnp.float32
                )
                place = lax.broadcasted_iota(jnp.int32, (BLOCK, half), 0)
                s = jnp.where(place <= lim_at(n, lanes), s, NEG)
                sbuf[n, :, lanes] = s
                most_here = jnp.max(s.reshape(BLOCK // 8, 8, half), axis=0)
                top = most_here if top is None else jnp.maximum(top, most_here)
            m = jnp.maximum(jnp.max(top, axis=0, keepdims=True), FLOOR)
            shift = m * const
            total = jnp.zeros((8, half), jnp.float32)
            for n in range(count):
                p = jnp.exp2(sbuf[n, :, lanes] * const - shift)
                total = total + jnp.sum(p.reshape(BLOCK // 8, 8, half), axis=0)
                wts[n * BLOCK : (n + 1) * BLOCK, lanes] = p.astype(jnp.bfloat16)
            l = jnp.sum(total, axis=0, keepdims=True)
            o = jnp.dot(vt_at(), wts[: count * BLOCK, lanes], preferred_element_type=jnp.float32)
            yield lanes, o, m, l

    def merge(j, h, lanes, o, m, l, scale_o):
        om, ol = stat[j, h, 0:1, lanes], stat[j, h, 1:2, lanes]
        top = jnp.maximum(m, om)
        f_new = jnp.exp2((m - top) * const)
        f_old = jnp.exp2((om - top) * const)
        part[j, h, :, lanes] = part[j, h, :, lanes] * f_old + o * (f_new * scale_o)
        stat[j, h, 0:1, lanes] = top
        stat[j, h, 1:2, lanes] = ol * f_old + l * f_new

    def put(j, h, results):
        for lanes, o, m, l in results:
            part[j, h, :, lanes] = o
            stat[j, h, 0:1, lanes] = m
            stat[j, h, 1:2, lanes] = l

    lag = 2
    pass_on(0)

    @pl.loop(0, heads + lag)
    def _(step):
        @pl.when(step < heads)
        def _():
            h = step

            for j in range(3):
                local(j, h).wait()
            k_side(h).wait_recv()
            v_side(h).wait_recv()

            vt[...] = vbuf[h].T

            @pl.loop(0, depth)
            def _(j):
                far = 2 * j + c > reach

                def block(first):
                    return lambda n: kbuf[h, (first + n) * BLOCK : (first + n + 1) * BLOCK, :]

                @pl.when(valid(j) & jnp.logical_not(far))
                def _():
                    put(j, h, piece(
                        j, h, block(0), lambda: vt[...], lambda n, lanes: lim[j, n, :, lanes], 2 * nb
                    ))

                if 2 * depth - 1 > reach:

                    @pl.when(valid(j) & far)
                    def _():
                        put(j, h, piece(
                            j, h, block(nb), lambda: vt[:, rows:],
                            lambda n, lanes: lim[j, nb + n, :, lanes], nb
                        ))

        @pl.when(step + 2 < heads)
        def _():
            give_own(step + 2)

        @pl.when(step + 1 < heads)
        def _():
            pass_on(step + 1)

        if ahead:
            hf = jnp.where(below(0), step - lag, step)

            @pl.when(takes & (hf >= 0) & (hf < heads))
            def _():
                k_look(hf).wait_recv()
                v_look(hf).wait_recv()
                vt[:, :look] = vla[hf].T
                for lanes, o, m, l in piece(
                    0, hf, lambda n: kla[hf, n * BLOCK : (n + 1) * BLOCK, :], lambda: vt[:, :look],
                    lambda n, lanes: limla[n, :, lanes], look // BLOCK
                ):
                    merge(0, hf, lanes, o, m, l, 1.0)

        @pl.loop(0, depth)
        def _(turn):
            j = depth - 1 - turn
            hf = jnp.where(below(j), step - lag, step)

            @pl.when(valid(j) & (hf >= 0) & (hf < heads))
            def _():
                @pl.when(below(j))
                def _():
                    remote(acc_s.at[j, hf], acc_r.at[j, hf], o_s.at[j, hf], o_r.at[j, hf], down).wait_recv()
                    remote(st_s.at[j, hf], st_r.at[j, hf], s_s.at[j, hf], s_r.at[j, hf], down).wait_recv()
                    m, l = st_r[j, hf, 0:1], st_r[j, hf, 1:2]
                    merge(j, hf, slice(None), acc_r[j, hf].astype(jnp.float32), m, l, l)

                l = stat[j, hf, 1:2]
                o = (part[j, hf] * (1.0 / jnp.where(l > 0.0, l, 1.0))).astype(jnp.bfloat16)

                @pl.when(j == 0)
                def _():
                    att[hf] = o

                @pl.when(j > 0)
                def _():
                    acc_s[j, hf] = o
                    st_s[j, hf] = stat[j, hf]
                    o_up(j, hf).start()
                    s_up(j, hf).start()

    w_copy.wait()
    attq[...] = att[...].reshape(heads * HEAD_DIM, rows).T
    wide = pbuf.shape[2]
    piece_rows = pbuf.shape[1]
    chunks = keep.shape[0]

    def to_mate(n):
        return remote(send1.at[n], recv1.at[n], e1s.at[n], e1r.at[n], mate)

    def to_across(n):
        return remote(send2.at[n], recv2.at[n], e2s.at[n], e2r.at[n], across)

    def span(n):
        return pl.ds(pl.multiple_of(n * wide, wide), wide)

    @pl.loop(0, chunks + 1)
    def _(step):
        @pl.when(step < chunks)
        def _():
            n = step
            full = jnp.dot(attq[...], wbuf[:, span(n)], preferred_element_type=jnp.float32)
            pbuf[...] = full.reshape(4, piece_rows, wide)
            for t in range(2):
                send1[n, t] = pbuf[2 * t + 1 - core].astype(jnp.bfloat16)
                keep[n, t] = pbuf[2 * t + core]
            to_mate(n).start()

        @pl.when(step > 0)
        def _():
            n = step - 1
            to_mate(n).wait_recv()
            far = keep[n, 1 - a] + recv1[n, 1 - a].astype(jnp.float32)
            send2[n] = far.astype(jnp.bfloat16)
            to_across(n).start()

    @pl.loop(0, chunks)
    def _(n):
        to_across(n).wait_recv()
        near = keep[n, a] + recv1[n, a].astype(jnp.float32) + recv2[n].astype(jnp.float32)
        out_ref[:, span(n)] = near.astype(out_ref.dtype)

    @pl.loop(0, chunks)
    def _(n):
        to_mate(n).wait_send()
        to_across(n).wait_send()

    @pl.loop(0, heads)
    def _(h):
        k_side(h).wait_send()
        v_side(h).wait_send()

        @pl.when(below(0))
        def _():
            q_own(h).wait_send()

        if ahead:

            @pl.when(gives)
            def _():
                k_look(h).wait_send()
                v_look(h).wait_send()

        @pl.loop(1, depth)
        def _(j):
            @pl.when(valid(j))
            def _():
                o_up(j, h).wait_send()
                s_up(j, h).wait_send()

                @pl.when(below(j))
                def _():
                    q_pass(j, h).wait_send()


def solution(mesh):
    n_ctx, n_tp = mesh.shape["ctx"], mesh.shape["tp"]

    def per_device(queries, keys, values, doc_ids, span_start, span_end, out_weight):
        rows, width = queries.shape
        heads = width // HEAD_DIM
        blocks = doc_ids.shape[0]
        nb = rows // BLOCK
        longest = blocks * 5 // 8
        reach = min(-(-(longest - 1) // nb), n_ctx - 1)
        levels = n_ctx // 2
        depth = min((reach + 1) // 2, levels - 1) + 1
        model = out_weight.shape[1]
        chunks = TAIL
        wide = model // chunks
        piece = rows // n_tp
        bf, f32, i32 = jnp.bfloat16, jnp.float32, jnp.int32
        dma = pltpu.SemaphoreType.DMA
        look = 3 * BLOCK
        smem = pl.BlockSpec(memory_space=pltpu.SMEM)
        anym = pl.BlockSpec(memory_space=pl.ANY)
        flops = 4 * rows * rows * 2 * width * depth + 2 * rows * width * model
        def attend(depth, ahead, ident):
            return pl.pallas_call(
                functools.partial(kernel, levels, reach, ahead),
                out_shape=jax.ShapeDtypeStruct((piece, model), bf),
                in_specs=[smem, smem, smem, anym, anym, anym, anym],
                out_specs=pl.BlockSpec(memory_space=pltpu.VMEM),
                scratch_shapes=[
                    pltpu.VMEM((depth, heads, rows, HEAD_DIM), bf),
                    pltpu.VMEM((heads, 2 * rows, HEAD_DIM), bf),
                    pltpu.VMEM((heads, 2 * rows, HEAD_DIM), bf),
                    pltpu.VMEM((heads, look, HEAD_DIM), bf),
                    pltpu.VMEM((heads, look, HEAD_DIM), bf),
                    pltpu.VMEM((depth, 2 * nb, 1, rows), i32),
                    pltpu.VMEM((3, 1, rows), i32),
                    pltpu.VMEM((depth, heads, HEAD_DIM, rows), f32),
                    pltpu.VMEM((depth, heads, 8, rows), f32),
                    pltpu.VMEM((depth, heads, HEAD_DIM, rows), bf),
                    pltpu.VMEM((depth, heads, HEAD_DIM, rows), bf),
                    pltpu.VMEM((depth, heads, 8, rows), f32),
                    pltpu.VMEM((depth, heads, 8, rows), f32),
                    pltpu.VMEM((heads, HEAD_DIM, rows), bf),
                    pltpu.VMEM((rows, width), bf),
                    pltpu.VMEM(out_weight.shape, bf),
                    pltpu.VMEM((4, piece, wide), f32),
                    pltpu.VMEM((chunks, 2, piece, wide), f32),
                    pltpu.VMEM((chunks, 2, piece, wide), bf),
                    pltpu.VMEM((chunks, 2, piece, wide), bf),
                    pltpu.VMEM((chunks, piece, wide), bf),
                    pltpu.VMEM((chunks, piece, wide), bf),
                    pltpu.VMEM((2 * nb, BLOCK, rows), f32),
                    pltpu.VMEM((2 * rows, rows), bf),
                    pltpu.VMEM((HEAD_DIM, 2 * rows), bf),
                    dma((depth, heads)), dma((depth, heads)),
                    dma((2, heads)), dma((2, heads)),
                    dma((2, heads)), dma((2, heads)),
                    dma((depth, heads)), dma((depth, heads)),
                    dma((depth, heads)), dma((depth, heads)),
                    dma((3, heads)), dma,
                    dma((chunks,)), dma((chunks,)),
                    dma((chunks,)), dma((chunks,)),
                ],
                compiler_params=pltpu.CompilerParams(
                    collective_id=ident, has_side_effects=True, vmem_limit_bytes=60 * 1024 * 1024
                ),
                cost_estimate=pl.CostEstimate(
                    flops=flops, bytes_accessed=8 * 1024 * 1024, transcendentals=0
                ),
            )

        level = jnp.arange(blocks, dtype=jnp.int32) // (2 * nb)
        same = doc_ids[:, None] == doc_ids[None, :]
        farthest = jnp.max(jnp.where(same, level[:, None] - level[None, :], 0))
        crossing = jnp.any(span_start // (2 * nb) != (span_end - 1) // (2 * nb))
        which = jnp.where(crossing, 0, jnp.where(farthest < depth - 1, 2, 1))
        return lax.switch(
            which,
            [attend(depth, True, 0), attend(depth, False, 1), attend(max(depth - 1, 1), False, 2)],
            doc_ids, span_start, span_end, queries, keys, values, out_weight,
        )


    return jax.shard_map(
        per_device,
        mesh=mesh,
        in_specs=(P("ctx", "tp"), P("ctx", "tp"), P("ctx", "tp"), P(), P(), P(), P("tp", None)),
        out_specs=P(("ctx", "tp"), None),
        check_vma=False,
    )
```
